32 devices in a mesh: ctx: 4 (over y, x), tp: 8 (over z, core).
Axes of the slice: x: 2, y: 2, z: 4, core: 2. Of those that a mesh axis runs over, the one named last changes fastest.
Arguments:
- x_input: bfloat16 [1024, 4096], P('ctx', 'tp'), may hold values from -6 to 6
- z_input: bfloat16 [1024, 4096], P('ctx', 'tp'), may hold values from -6 to 6
- bc_input: bfloat16 [1024, 1024], P('ctx', 'tp'), may hold values from -6 to 6
- dt_input: float32 [1024, 64], P('ctx', 'tp'), may hold values from -6 to 6
- decay_log: float32 [64], P('tp'), may hold values from -12 to -2
- skip_weight: float32 [64], P('tp'), may hold values from 0.5 to 2
- conv_x: float32 [4, 4096], P(None, 'tp'), may hold values from -3 to 3
- conv_bc: float32 [4, 1024], replicated, may hold values from -3 to 3
- conv_bias_x: float32 [4096], P('tp'), may hold values from -3 to 3
- conv_bias_bc: float32 [1024], replicated, may hold values from -3 to 3
- norm_gain: float32 [4096], P('tp'), may hold values from 0.1 to 1.9
- out_weight: bfloat16 [4096, 8192], P('tp'), may hold values from -0.09375 to 0.09375
Outputs:
- mixed: bfloat16 [1024, 8192], P('ctx', 'tp')
The draws below stay inside these ranges and needn't reach their ends.
All inputs are finite; a program needn't handle non-finite values.
Results may differ from the reference program's by a relative error of at most 0.0055.
Values may be sent and summed in bfloat16 or wider, within the bound.
A program may use at most 128 MiB of HBM per device.

```python
import math
import jax
import jax.numpy as jnp
from jax import lax

D = 8192
HEAD = 64
STATE = 128
KERNEL = 4
TOK_DEV = 256
HEADS = 64
GROUPS = 4
INNER = 4096
SEQ = 1024


def draw_decay_log(key, part):
    first_key, second_key, third_key = jax.random.split(jax.random.fold_in(key, 17), 3)
    share = 0.5
    slow_low, slow_high = (0.3, 1.5)
    quick_heads = jax.random.uniform(first_key, (HEADS,), jnp.float32) < share
    quick = jax.random.uniform(second_key, (HEADS,), jnp.float32, math.log(0.03), math.log(0.06))
    slow = jnp.log(jax.random.uniform(third_key, (HEADS,), jnp.float32, slow_low, slow_high) / SEQ)
    return jnp.where(quick_heads, quick, slow).astype(jnp.float32)


def draw_dt_input(key, part):
    level_key, head_key, noise_key = jax.random.split(jax.random.fold_in(key, 29), 3)
    block_count = SEQ // TOK_DEV
    level = jax.random.uniform(level_key, (block_count, 1), jnp.float32, -2.5, 2.5)
    head_level = jax.random.uniform(head_key, (block_count, HEADS), jnp.float32, -0.5, 0.5)
    offsets = jnp.repeat(level + head_level, TOK_DEV, axis=0)
    noise = jax.random.normal(noise_key, (SEQ, HEADS), jnp.float32)
    return jnp.clip(offsets + noise, -6.0, 6.0).astype(jnp.float32)


def shard_levels(rng, extent, cuts, low, top_value):
    gain, own = 1.0, jax.random.fold_in(rng, 6)
    for axis_at, parts in cuts:
        draws = jnp.exp(jax.random.uniform(jax.random.fold_in(own, axis_at), (parts,), jnp.float32, low / len(cuts), top_value / len(cuts)))
        gain = gain * jnp.repeat(draws, extent[axis_at] // parts).reshape([-1 if axis == axis_at else 1 for axis in range(len(extent))])
    return gain


def centred(own_key, extent, scale, most, cuts=(), kind=jnp.bfloat16):
    level = shard_levels(own_key, extent, cuts, -0.22, 0.18) if cuts else 1.0
    values = jax.random.normal(own_key, extent, jnp.float32) * scale * level
    return jnp.minimum(jnp.maximum(values, -most), most).astype(kind)


def setup_inputs(seed: int = 0) -> dict:
    key_of = jax.random.split(jax.random.key(seed), 13)
    return {
        "x_input": centred(key_of[0], (SEQ, INNER), 1.0, 6.0, ((0, 4), (1, 8))),
        "z_input": centred(key_of[1], (SEQ, INNER), 1.0, 6.0, ((0, 4), (1, 8))),
        "bc_input": centred(key_of[2], (SEQ, 2 * GROUPS * STATE), 1.0, 6.0, ((0, 4), (1, 8))),
        "dt_input": draw_dt_input(jax.random.fold_in(key_of[12], 71), 0),
        "decay_log": draw_decay_log(jax.random.fold_in(key_of[12], 71), 0),
        "skip_weight": jnp.clip(jnp.exp(math.log(2.0) - 1.3862944 * jax.random.uniform(key_of[5], (HEADS,), jnp.float32) ** shard_levels(key_of[5], (HEADS,), ((0, 8),), -0.2, 0.2)), 0.5, 2.0),
        "conv_x": centred(key_of[6], (KERNEL, INNER), KERNEL ** -0.5, 3.0, ((1, 8),), jnp.float32),
        "conv_bc": centred(key_of[7], (KERNEL, 2 * GROUPS * STATE), KERNEL ** -0.5, 3.0, (), jnp.float32),
        "conv_bias_x": centred(key_of[8], (INNER,), 0.5, 3.0, ((0, 8),), jnp.float32),
        "conv_bias_bc": centred(key_of[9], (2 * GROUPS * STATE,), 0.5, 3.0, (), jnp.float32),
        "norm_gain": jnp.clip(1.0 + 0.18 * jax.random.normal(key_of[10], (INNER,), jnp.float32), 0.1, 1.9),
        "out_weight": centred(key_of[11], (INNER, D), INNER ** -0.5, 0.09375, ((0, 8),)),
    }


HIGH = lax.Precision.HIGHEST

def causal_conv(raw, kernel, offset):
    values = raw.astype(jnp.float32)
    reach = kernel.shape[0] - 1
    padded = jnp.concatenate([jnp.zeros((reach, values.shape[1]), jnp.float32), values], axis=0)
    length = values.shape[0]
    total = offset[None, :] + kernel[0][None, :] * padded[0:length]
    for step in range(1, kernel.shape[0]):
        total = total + kernel[step][None, :] * padded[step:step + length]
    return jax.nn.silu(total)

def reference(x_input, z_input, bc_input, dt_input, decay_log, skip_weight, conv_x, conv_bc, conv_bias_x, conv_bias_bc, norm_gain, out_weight):
    xs = causal_conv(x_input, conv_x, conv_bias_x)
    bcs = causal_conv(bc_input, conv_bc, conv_bias_bc).reshape(SEQ, GROUPS, 2, STATE)
    b_all = bcs[:, :, 0, :]
    c_all = bcs[:, :, 1, :]
    step_size = jax.nn.softplus(dt_input)
    decay_rate = -jnp.exp(decay_log)
    per_group = HEADS // GROUPS
    heads_x = xs.reshape(SEQ, HEADS, HEAD)
    blocks = SEQ // TOK_DEV
    lower = jnp.tril(jnp.ones((TOK_DEV, TOK_DEV), dtype=bool))

    def split_blocks(array):
        return array.reshape((blocks, TOK_DEV) + array.shape[1:])

    def block_step(state, pieces):
        block_x, block_b, block_c, block_dt = pieces
        running = jnp.cumsum(block_dt * decay_rate[None, :], axis=0)
        intersection = jnp.einsum('tgn,sgn->gts', block_c, block_b, precision=HIGH)
        intersection = jnp.repeat(intersection, per_group, axis=0)
        gap = running.T[:, :, None] - running.T[:, None, :]
        weights = jnp.where(lower[None], jnp.exp(jnp.minimum(gap, 0.0)), 0.0) * intersection * block_dt.T[:, None, :]
        local_out = jnp.einsum('hts,shp->thp', weights, block_x, precision=HIGH)
        head_b = jnp.repeat(block_b, per_group, axis=1)
        head_c = jnp.repeat(block_c, per_group, axis=1)
        carried = jnp.einsum('thn,hpn->thp', head_c, state, precision=HIGH) * jnp.exp(running)[:, :, None]
        output = local_out + carried + skip_weight[None, :, None] * block_x
        closing = jnp.exp(running[-1][None, :] - running) * block_dt
        local_state = jnp.einsum('sh,shp,shn->hpn', closing, block_x, head_b, precision=HIGH)
        new_state = jnp.exp(running[-1])[:, None, None] * state + local_state
        return (new_state, output)
    start_state = jnp.zeros((HEADS, HEAD, STATE), jnp.float32)
    ignored, outputs = lax.scan(block_step, start_state, (split_blocks(heads_x), split_blocks(b_all), split_blocks(c_all), split_blocks(step_size)))
    ssm_out = outputs.reshape(SEQ, INNER)
    gated = ssm_out * jax.nn.silu(z_input.astype(jnp.float32))
    meansq = lax.optimization_barrier(jnp.mean(gated * gated, axis=1))
    hidden = (gated * norm_gain[None, :]).astype(jnp.bfloat16)
    projected = jnp.dot(hidden, out_weight, preferred_element_type=jnp.float32)
    return (projected * lax.rsqrt(meansq + 1e-05)[:, None]).astype(jnp.bfloat16)
```

```python
import functools

import jax
import jax.numpy as jnp
from jax import lax
from jax.experimental import pallas as pl
from jax.experimental.pallas import tpu as pltpu
from jax.sharding import PartitionSpec as P

MESH = pl.DeviceIdType.MESH
HIGH = lax.Precision.HIGHEST
F32 = jnp.float32
BF16 = jnp.bfloat16
HALO = 16
CHUNKS = 4


def dot(a, b, precision=None):
    return jnp.dot(a, b, preferred_element_type=F32, precision=precision)


def silu(v):
    return v / (1.0 + jnp.exp(-v))


def split(v):
    high = v.astype(BF16)
    return high, (v - high.astype(F32)).astype(BF16)


def layer_kernel(
    n_ctx,
    n_tp,
    x_ref,
    z_ref,
    bc_ref,
    dt_ref,
    decay_ref,
    skip_ref,
    conv_x_ref,
    conv_bc_ref,
    bias_x_ref,
    bias_bc_ref,
    gain_ref,
    w_ref,
    out_ref,
    halo_x,
    halo_bc,
    raw_bc,
    pad_x,
    pad_bc,
    xs,
    y,
    grown,
    state_own,
    carry_own,
    state_in,
    carry_in,
    incoming,
    squares,
    hid_own,
    hid_sib,
    w_own,
    w_sib,
    acc,
    outgoing,
    arrived,
    halo_send,
    halo_recv,
    state_send,
    state_recv,
    square_send,
    square_recv,
    hid_sem,
    w_local,
    w_send,
    w_recv,
    block_send,
    block_recv,
):
    ctx = lax.axis_index("ctx")
    rank = lax.axis_index("tp")
    zed = rank // 2
    core = rank % 2
    sib = rank + 1 - 2 * core
    n_z = n_tp // 2
    length, inner = x_ref.shape
    size = bc_ref.shape[1]
    heads = dt_ref.shape[1]
    taps = conv_x_ref.shape[0]
    width = w_own.shape[2]
    rows = length // CHUNKS
    wide = 2 * (inner // heads)

    barrier = pltpu.get_barrier_semaphore()

    def greet(c, r):
        pl.semaphore_signal(barrier, inc=1, device_id=(c, r), device_id_type=MESH)

    for step in range(1, n_tp):
        greet(ctx, lax.rem(rank + step, n_tp))
    for step in range(1, n_ctx):
        greet(lax.rem(ctx + step, n_ctx), rank)
    greet(lax.rem(ctx + 1, n_ctx), sib)
    greet(lax.rem(ctx + n_ctx - 1, n_ctx), sib)

    def w_block(block, half):
        return w_ref.at[:, pl.ds(pl.multiple_of((2 * block + half) * width, width), width)]

    def remote(src, dst, send, recv, c, r):
        return pltpu.make_async_remote_copy(
            src_ref=src,
            dst_ref=dst,
            send_sem=send,
            recv_sem=recv,
            device_id=(c, r),
            device_id_type=MESH,
        )

    local_w = [
        pltpu.make_async_copy(w_block(b, core), w_own.at[b], w_local.at[b]) for b in range(n_z)
    ]
    pl.semaphore_wait(barrier, (n_tp - 1) + (n_ctx - 1) + 2)

    later = lax.rem(ctx + 1, n_ctx)
    tail = pl.ds(length - HALO, HALO)
    x_halo = remote(
        x_ref.at[tail], halo_x, halo_send.at[0], halo_recv.at[0], later, rank
    )
    bc_halo = remote(
        bc_ref.at[tail], halo_bc.at[core], halo_send.at[1], halo_recv.at[1 + core], later, rank
    )
    bc_halo_sib = remote(
        bc_ref.at[tail], halo_bc.at[core], halo_send.at[2], halo_recv.at[1 + core], later, sib
    )
    bc_swap = remote(
        bc_ref, raw_bc.at[core], halo_send.at[3], halo_recv.at[3], ctx, sib
    )

    @pl.when(ctx < n_ctx - 1)
    def _():
        x_halo.start()
        bc_halo.start()
        bc_halo_sib.start()

    bc_swap.start()
    sent_w = [
        remote(w_block(b, 1 - core), w_sib.at[b], w_send.at[b], w_recv.at[b], ctx, sib)
        for b in range(n_z)
    ]
    for b in range(n_z):
        sent_w[b].start()
        local_w[b].start()
    raw_bc[core] = bc_ref[...]

    logits = dt_ref[...].T
    step_size = jnp.maximum(logits, 0.0) + jnp.log(1.0 + jnp.exp(-jnp.abs(logits)))
    rate = -jnp.exp(decay_ref[...])
    earlier = lax.broadcasted_iota(jnp.int32, (length, length), 0)
    after = lax.broadcasted_iota(jnp.int32, (length, length), 1)
    upper = jnp.where(earlier <= after, 1.0, 0.0).astype(F32)
    running = dot(step_size * rate, upper, HIGH)
    total = running[:, length - 1 : length]
    closing = jnp.exp(total - running) * step_size
    running_col = running.T
    closing_col = closing.T
    grown_col = jnp.exp(running_col)
    last_col = grown_col[length - 1 : length, :]
    lane = lax.broadcasted_iota(jnp.int32, (1, wide), 1)
    first = lane < wide // 2

    def spread(cols, pair):
        return jnp.where(
            first, cols[:, 2 * pair : 2 * pair + 1], cols[:, 2 * pair + 1 : 2 * pair + 2]
        )

    pairs = heads // 2
    for p in range(pairs):
        at = slice(p * wide, (p + 1) * wide)
        grown[:, at] = spread(grown_col, p)
        carry_own[:, at] = jnp.broadcast_to(spread(last_col, p), (8, wide))

    @pl.when(ctx == 0)
    def _():
        halo_x[...] = jnp.zeros_like(halo_x)
        halo_bc[...] = jnp.zeros_like(halo_bc)

    @pl.when(ctx > 0)
    def _():
        x_halo.wait_recv()

    def conv(pad, kernel, bias):
        value = bias
        for k in range(taps):
            start = HALO - (taps - 1) + k
            value = value + kernel[k : k + 1, :] * pad[start : start + length, :]
        return silu(value)

    pad_x[0:HALO, :] = halo_x[...].astype(F32)
    pad_x[HALO:, :] = x_ref[...].astype(F32)
    xs[...] = conv(pad_x, conv_x_ref[...], bias_x_ref[...])

    @pl.when(ctx > 0)
    def _():
        for half in range(2):
            pltpu.make_async_copy(
                halo_bc.at[half], halo_bc.at[half], halo_recv.at[1 + half]
            ).wait()

    bc_swap.wait_recv()
    for half in range(2):
        at = slice(half * size, (half + 1) * size)
        pad_bc[0:HALO, at] = halo_bc[half].astype(F32)
        pad_bc[HALO:, at] = raw_bc[half].astype(F32)
    group = pl.ds(pl.multiple_of(zed * 2 * size, 2 * size), 2 * size)
    bcs = conv(pad_bc, conv_bc_ref[:, group], bias_bc_ref[:, group])
    b_mat = bcs[:, :size]
    c_mat = bcs[:, size:]

    b_turned = b_mat.T.astype(BF16)
    for p in range(pairs):
        at = slice(p * wide, (p + 1) * wide)
        scaled = (xs[:, at] * spread(closing_col, p)).astype(BF16)
        state_own[:, at] = dot(b_turned, scaled).astype(BF16)

    def state_copies(target):
        return (
            remote(
                state_own,
                state_in.at[ctx],
                state_send.at[0, target],
                state_recv.at[0, ctx],
                target,
                rank,
            ),
            remote(
                carry_own,
                carry_in.at[ctx],
                state_send.at[1, target],
                state_recv.at[1, ctx],
                target,
                rank,
            ),
        )

    for target in range(1, n_ctx):

        @pl.when(target > ctx)
        def _():
            for copy in state_copies(target):
                copy.start()

    meeting = lax.dot_general(
        c_mat, b_mat, (((1,), (1,)), ((), ())), preferred_element_type=F32, precision=HIGH
    )
    meeting = jnp.where(earlier >= after, meeting, 0.0)
    for p in range(pairs):
        at = slice(p * wide, (p + 1) * wide)
        values = xs[:, at]
        high, low = split(values)
        both = jnp.concatenate([high, low], axis=1)
        parts = []
        for h in (2 * p, 2 * p + 1):
            gap = running_col[:, h : h + 1] - running[h : h + 1, :]
            weights = jnp.exp(jnp.minimum(gap, 0.0)) * meeting * step_size[h : h + 1, :]
            product = dot(weights.astype(BF16), both)
            parts.append(product[:, :wide] + product[:, wide:])
        y[:, at] = jnp.where(first, parts[0], parts[1]) + values * jnp.where(
            first, skip_ref[0, 2 * p], skip_ref[0, 2 * p + 1]
        )
    gate = silu(z_ref[...].astype(F32))

    incoming[...] = jnp.zeros_like(incoming)
    for source in range(n_ctx - 1):

        @pl.when(source < ctx)
        def _():
            pltpu.make_async_copy(
                state_in.at[source], state_in.at[source], state_recv.at[0, source]
            ).wait()
            pltpu.make_async_copy(
                carry_in.at[source], carry_in.at[source], state_recv.at[1, source]
            ).wait()
            incoming[...] = incoming[...] * carry_in[source, 0:1, :] + state_in[source].astype(F32)

    c_high, c_low = split(c_mat)
    state = incoming[...].astype(BF16)
    carried = dot(
        jnp.concatenate([c_high, c_low], axis=1), jnp.concatenate([state, state], axis=0)
    )
    gated = (y[...] + carried * grown[...]) * gate
    hid_own[...] = (gated * gain_ref[...]).astype(BF16)
    hid_swap = remote(hid_own, hid_sib, hid_sem.at[0], hid_sem.at[1], ctx, sib)
    hid_swap.start()
    norm = jnp.sum(gated * gated, axis=1, keepdims=True)
    squares[rank] = jnp.broadcast_to(norm, (length, 128)).T[0:8, :]

    def square_copy(target):
        return remote(
            squares.at[rank],
            squares.at[rank],
            square_send.at[target],
            square_recv.at[rank],
            ctx,
            target,
        )

    for target in range(n_tp):

        @pl.when(target != rank)
        def _():
            square_copy(target).start()

    def part(r):
        return pl.ds(r * rows, rows)

    def block_copy(target, r, forward):
        if forward:
            slot, to = target, rank + 2
        else:
            slot, to = jnp.where(target == zed - 1, n_z, target), rank - 2
        return remote(
            outgoing.at[target, part(r)],
            arrived.at[slot, part(r)],
            block_send.at[target, r],
            block_recv.at[slot, r],
            ctx,
            to,
        )

    def block_wait(slot, r):
        pltpu.make_async_copy(
            arrived.at[slot, part(r)], arrived.at[slot, part(r)], block_recv.at[slot, r]
        ).wait()

    for b in range(n_z):
        local_w[b].wait()
        sent_w[b].wait_recv()
    hid_swap.wait_recv()

    upward = zed < n_z // 2
    for i in range(n_z):
        target = jnp.where(upward, n_z - 1 - i, i)
        total_block = dot(hid_own[...], w_own[target]) + dot(hid_sib[...], w_sib[target])
        acc[target] = total_block

        if i < n_z - 1:

            @pl.when((zed == 0) | (zed == n_z - 1))
            def _():
                outgoing[target] = acc[target].astype(BF16)

            @pl.when(zed == 0)
            def _():
                for r in range(CHUNKS):
                    block_copy(target, r, True).start()

            @pl.when(zed == n_z - 1)
            def _():
                for r in range(CHUNKS):
                    block_copy(target, r, False).start()

    def relay(target, r, forward):
        block_wait(target, r)
        outgoing[target, part(r)] = (
            acc[target, part(r)] + arrived[target, part(r)].astype(F32)
        ).astype(BF16)
        block_copy(target, r, forward).start()

    for i in range(n_z - 1):
        for r in range(CHUNKS):

            @pl.when((zed > 0) & (zed < n_z - 1 - i))
            def _():
                relay(n_z - 1 - i, r, True)

            @pl.when((zed < n_z - 1) & (zed > i))
            def _():
                relay(i, r, False)

    for target in range(n_tp):

        @pl.when(target != rank)
        def _():
            pltpu.make_async_copy(
                squares.at[target], squares.at[target], square_recv.at[target]
            ).wait()

    mean = jnp.sum(squares[...], axis=0) * (1.0 / (inner * n_tp))
    scale = lax.rsqrt(mean + 1e-05).T[:, 0:1]
    for r in range(CHUNKS):

        @pl.when(zed < n_z - 1)
        def _():
            block_wait(n_z, r)
            acc[zed, part(r)] = acc[zed, part(r)] + arrived[n_z, part(r)].astype(F32)

        @pl.when(zed > 0)
        def _():
            block_wait(zed, r)
            acc[zed, part(r)] = acc[zed, part(r)] + arrived[zed, part(r)].astype(F32)

        out_ref[part(r), :] = (
            acc[zed, part(r)] * scale[r * rows : (r + 1) * rows, :]
        ).astype(BF16)

    @pl.when(ctx < n_ctx - 1)
    def _():
        x_halo.wait_send()
        bc_halo.wait_send()
        bc_halo_sib.wait_send()

    bc_swap.wait_send()
    for copy in sent_w:
        copy.wait_send()
    for target in range(1, n_ctx):

        @pl.when(target > ctx)
        def _():
            for copy in state_copies(target):
                copy.wait_send()

    hid_swap.wait_send()
    for target in range(n_tp):

        @pl.when(target != rank)
        def _():
            square_copy(target).wait_send()

    for target in range(n_z):
        for r in range(CHUNKS):

            @pl.when(zed != target)
            def _():
                pltpu.make_async_copy(
                    outgoing.at[target, part(r)],
                    outgoing.at[target, part(r)],
                    block_send.at[target, r],
                ).wait()


def solution(mesh):
    n_ctx, n_tp = mesh.shape["ctx"], mesh.shape["tp"]
    n_z = n_tp // 2

    def shards(
        x_input,
        z_input,
        bc_input,
        dt_input,
        decay_log,
        skip_weight,
        conv_x,
        conv_bc,
        conv_bias_x,
        conv_bias_bc,
        norm_gain,
        out_weight,
    ):
        length, inner = x_input.shape
        size = bc_input.shape[1]
        heads = dt_input.shape[1]
        features = out_weight.shape[1]
        width = features // n_tp
        vmem = pl.BlockSpec(memory_space=pltpu.VMEM)
        smem = pl.BlockSpec(memory_space=pltpu.SMEM)
        hbm = pl.BlockSpec(memory_space=pl.ANY)
        dma = pltpu.SemaphoreType.DMA
        return pl.pallas_call(
            functools.partial(layer_kernel, n_ctx, n_tp),
            out_shape=jax.ShapeDtypeStruct((length, width), BF16),
            in_specs=[vmem, vmem, vmem, vmem, vmem, smem, vmem, vmem, vmem, vmem, vmem, hbm],
            out_specs=vmem,
            scratch_shapes=[
                pltpu.VMEM((HALO, inner), BF16),
                pltpu.VMEM((2, HALO, size), BF16),
                pltpu.VMEM((2, length, size), BF16),
                pltpu.VMEM((HALO + length, inner), F32),
                pltpu.VMEM((HALO + length, 2 * size), F32),
                pltpu.VMEM((length, inner), F32),
                pltpu.VMEM((length, inner), F32),
                pltpu.VMEM((length, inner), F32),
                pltpu.VMEM((size, inner), BF16),
                pltpu.VMEM((8, inner), F32),
                pltpu.VMEM((n_ctx, size, inner), BF16),
                pltpu.VMEM((n_ctx, 8, inner), F32),
                pltpu.VMEM((size, inner), F32),
                pltpu.VMEM((n_tp, 8, length), F32),
                pltpu.VMEM((length, inner), BF16),
                pltpu.VMEM((length, inner), BF16),
                pltpu.VMEM((n_z, inner, width), BF16),
                pltpu.VMEM((n_z, inner, width), BF16),
                pltpu.VMEM((n_z, length, width), F32),
                pltpu.VMEM((n_z, length, width), BF16),
                pltpu.VMEM((n_z + 1, length, width), BF16),
                dma((4,)),
                dma((4,)),
                dma((2, n_ctx)),
                dma((2, n_ctx)),
                dma((n_tp,)),
                dma((n_tp,)),
                dma((2,)),
                dma((n_z,)),
                dma((n_z,)),
                dma((n_z,)),
                dma((n_z, CHUNKS)),
                dma((n_z + 1, CHUNKS)),
            ],
            compiler_params=pltpu.CompilerParams(
                collective_id=0, has_side_effects=True, vmem_limit_bytes=48 * 1024 * 1024
            ),
        )(
            x_input,
            z_input,
            bc_input,
            dt_input,
            decay_log.reshape(heads, 1),
            skip_weight.reshape(1, heads),
            conv_x,
            conv_bc,
            conv_bias_x.reshape(1, -1),
            conv_bias_bc.reshape(1, -1),
            norm_gain.reshape(1, -1),
            out_weight,
        )

    in_specs = (
        P("ctx", "tp"),
        P("ctx", "tp"),
        P("ctx", "tp"),
        P("ctx", "tp"),
        P("tp"),
        P("tp"),
        P(None, "tp"),
        P(),
        P("tp"),
        P(),
        P("tp"),
        P("tp", None),
    )
    return jax.shard_map(
        shards, mesh=mesh, in_specs=in_specs, out_specs=P("ctx", "tp"), check_vma=False
    )
```

```python
import functools

import jax
import jax.numpy as jnp
from jax import lax
from jax.experimental import pallas as pl
from jax.experimental.pallas import tpu as pltpu
from jax.sharding import PartitionSpec as P

MESH = pl.DeviceIdType.MESH
HIGH = lax.Precision.HIGHEST
F32 = jnp.float32
BF16 = jnp.bfloat16
HALO = 16
CHUNKS = 4
HALVES = 2


def dot(a, b, precision=None):
    return jnp.dot(a, b, preferred_element_type=F32, precision=precision)


def silu(v):
    return v / (1.0 + jnp.exp(-v))


def split(v):
    high = v.astype(BF16)
    return high, (v - high.astype(F32)).astype(BF16)


def layer_kernel(
    n_ctx,
    n_tp,
    x_hbm,
    z_hbm,
    bc_ref,
    dt_hbm,
    decay_hbm,
    skip_hbm,
    conv_x_hbm,
    conv_bc_hbm,
    bias_x_hbm,
    bias_bc_hbm,
    gain_hbm,
    w_ref,
    out_ref,
    x_ref,
    z_ref,
    dt_ref,
    decay_ref,
    skip_ref,
    conv_x_ref,
    conv_bc_ref,
    bias_x_ref,
    bias_bc_ref,
    gain_ref,
    fetch_sem,
    halo_x,
    halo_bc,
    raw_bc,
    pad_x,
    pad_bc,
    xs,
    y,
    grown,
    gate,
    c_pair,
    state_own,
    carry_own,
    state_in,
    carry_in,
    incoming,
    squares,
    hid_own,
    hid_sib,
    w_own,
    w_sib,
    acc,
    outgoing,
    arrived,
    halo_send,
    halo_recv,
    state_send,
    state_recv,
    square_send,
    square_recv,
    hid_send,
    hid_recv,
    w_local,
    w_send,
    w_recv,
    block_send,
    block_recv,
):
    ctx = lax.axis_index("ctx")
    rank = lax.axis_index("tp")
    zed = rank // 2
    core = rank % 2
    sib = rank + 1 - 2 * core
    n_z = n_tp // 2
    length, inner = x_ref.shape
    size = bc_ref.shape[1]
    heads = dt_ref.shape[0]
    taps = conv_x_ref.shape[0]
    width = w_own.shape[2]
    rows = length // CHUNKS
    wide = 2 * (inner // heads)

    group = pl.ds(pl.multiple_of(zed * 2 * size, 2 * size), 2 * size)
    fetched = {}
    for at, (name, src, dst) in enumerate(
        (
            ("dt", dt_hbm, dt_ref),
            ("decay", decay_hbm, decay_ref),
            ("x", x_hbm, x_ref),
            ("conv_x", conv_x_hbm, conv_x_ref),
            ("bias_x", bias_x_hbm, bias_x_ref),
            ("bc", bc_ref, raw_bc.at[core]),
            ("conv_bc", conv_bc_hbm.at[:, group], conv_bc_ref),
            ("bias_bc", bias_bc_hbm.at[:, group], bias_bc_ref),
            ("skip", skip_hbm, skip_ref),
            ("z", z_hbm, z_ref),
            ("gain", gain_hbm, gain_ref),
        )
    ):
        fetched[name] = pltpu.make_async_copy(src, dst, fetch_sem.at[at])

    barrier = pltpu.get_barrier_semaphore()

    def greet(c, r):
        pl.semaphore_signal(barrier, inc=1, device_id=(c, r), device_id_type=MESH)

    for step in range(1, n_tp):
        greet(ctx, lax.rem(rank + step, n_tp))
    for step in range(1, n_ctx):
        greet(lax.rem(ctx + step, n_ctx), rank)
    greet(lax.rem(ctx + 1, n_ctx), sib)
    greet(lax.rem(ctx + n_ctx - 1, n_ctx), sib)

    for copy in fetched.values():
        copy.start()

    def w_block(block, half):
        return w_ref.at[:, pl.ds(pl.multiple_of((2 * block + half) * width, width), width)]

    def remote(src, dst, send, recv, c, r):
        return pltpu.make_async_remote_copy(
            src_ref=src,
            dst_ref=dst,
            send_sem=send,
            recv_sem=recv,
            device_id=(c, r),
            device_id_type=MESH,
        )

    local_w = [
        pltpu.make_async_copy(w_block(b, core), w_own.at[b], w_local.at[b]) for b in range(n_z)
    ]
    pl.semaphore_wait(barrier, (n_tp - 1) + (n_ctx - 1) + 2)

    later = lax.rem(ctx + 1, n_ctx)
    tail = pl.ds(length - HALO, HALO)
    x_halo = remote(
        x_hbm.at[tail], halo_x, halo_send.at[0], halo_recv.at[0], later, rank
    )
    bc_halo = remote(
        bc_ref.at[tail], halo_bc.at[core], halo_send.at[1], halo_recv.at[1 + core], later, rank
    )
    bc_halo_sib = remote(
        bc_ref.at[tail], halo_bc.at[core], halo_send.at[2], halo_recv.at[1 + core], later, sib
    )
    bc_swap = remote(
        bc_ref, raw_bc.at[core], halo_send.at[3], halo_recv.at[3], ctx, sib
    )

    @pl.when(ctx < n_ctx - 1)
    def _():
        x_halo.start()
        bc_halo.start()
        bc_halo_sib.start()

    bc_swap.start()
    sent_w = [
        remote(w_block(b, 1 - core), w_sib.at[b], w_send.at[b], w_recv.at[b], ctx, sib)
        for b in range(n_z)
    ]
    for b in range(n_z):
        sent_w[b].start()
        local_w[b].start()

    fetched["dt"].wait()
    fetched["decay"].wait()
    logits = dt_ref[...]
    step_size = jnp.maximum(logits, 0.0) + jnp.log(1.0 + jnp.exp(-jnp.abs(logits)))
    head_row = lax.broadcasted_iota(jnp.int32, (heads, heads), 0)
    head_lane = lax.broadcasted_iota(jnp.int32, (heads, heads), 1)
    decay = jnp.where(head_row == head_lane, decay_ref[...], 0.0)
    rate = -jnp.exp(jnp.sum(decay, axis=1, keepdims=True))
    earlier = lax.broadcasted_iota(jnp.int32, (length, length), 0)
    after = lax.broadcasted_iota(jnp.int32, (length, length), 1)
    upper = jnp.where(earlier <= after, 1.0, 0.0).astype(F32)
    running = dot(step_size * rate, upper, HIGH)
    total = running[:, length - 1 : length]
    closing = jnp.exp(total - running) * step_size
    running_col = running.T
    closing_col = closing.T
    grown_col = jnp.exp(running_col)
    last_col = grown_col[length - 1 : length, :]
    lane = lax.broadcasted_iota(jnp.int32, (1, wide), 1)
    first = lane < wide // 2

    def spread(cols, pair):
        return jnp.where(
            first, cols[:, 2 * pair : 2 * pair + 1], cols[:, 2 * pair + 1 : 2 * pair + 2]
        )

    pairs = heads // 2
    for p in range(pairs):
        at = slice(p * wide, (p + 1) * wide)
        grown[:, at] = spread(grown_col, p)
        carry_own[:, at] = jnp.broadcast_to(spread(last_col, p), (8, wide))

    def conv(pad, kernel, bias, begin, end):
        value = bias
        for k in range(taps):
            start = HALO - (taps - 1) + k
            value = value + kernel[k : k + 1, :] * pad[start + begin : start + end, :]
        return silu(value)

    fetched["x"].wait()
    fetched["conv_x"].wait()
    fetched["bias_x"].wait()
    pad_x[HALO:, :] = x_ref[...].astype(F32)
    xs[HALO:, :] = conv(pad_x, conv_x_ref[...], bias_x_ref[...], HALO, length)

    @pl.when(ctx == 0)
    def _():
        halo_x[...] = jnp.zeros_like(halo_x)
        halo_bc[...] = jnp.zeros_like(halo_bc)

    @pl.when(ctx > 0)
    def _():
        x_halo.wait_recv()

    pad_x[0:HALO, :] = halo_x[...].astype(F32)
    xs[0:HALO, :] = conv(pad_x, conv_x_ref[...], bias_x_ref[...], 0, HALO)

    @pl.when(ctx > 0)
    def _():
        for half in range(2):
            pltpu.make_async_copy(
                halo_bc.at[half], halo_bc.at[half], halo_recv.at[1 + half]
            ).wait()

    fetched["bc"].wait()
    fetched["conv_bc"].wait()
    fetched["bias_bc"].wait()
    bc_swap.wait_recv()
    for half in range(2):
        at = slice(half * size, (half + 1) * size)
        pad_bc[0:HALO, at] = halo_bc[half].astype(F32)
        pad_bc[HALO:, at] = raw_bc[half].astype(F32)
    bcs = conv(pad_bc, conv_bc_ref[...], bias_bc_ref[...], 0, length)
    b_mat = bcs[:, :size]
    c_mat = bcs[:, size:]

    b_turned = b_mat.T.astype(BF16)
    for p in range(pairs):
        at = slice(p * wide, (p + 1) * wide)
        scaled = (xs[:, at] * spread(closing_col, p)).astype(BF16)
        state_own[:, at] = dot(b_turned, scaled).astype(BF16)

    def state_copies(target):
        return (
            remote(
                state_own,
                state_in.at[ctx],
                state_send.at[0, target],
                state_recv.at[0, ctx],
                target,
                rank,
            ),
            remote(
                carry_own,
                carry_in.at[ctx],
                state_send.at[1, target],
                state_recv.at[1, ctx],
                target,
                rank,
            ),
        )

    for target in range(1, n_ctx):

        @pl.when(target > ctx)
        def _():
            for copy in state_copies(target):
                copy.start()

    meeting = lax.dot_general(
        c_mat, b_mat, (((1,), (1,)), ((), ())), preferred_element_type=F32, precision=HIGH
    )
    fetched["skip"].wait()
    skips = skip_ref[...]
    meeting = jnp.where(earlier >= after, meeting, 0.0)
    for p in range(pairs):
        at = slice(p * wide, (p + 1) * wide)
        values = xs[:, at]
        high, low = split(values)
        both = jnp.concatenate([high, low], axis=1)
        parts = []
        for h in (2 * p, 2 * p + 1):
            gap = running_col[:, h : h + 1] - running[h : h + 1, :]
            weights = jnp.exp(jnp.minimum(gap, 0.0)) * meeting * step_size[h : h + 1, :]
            product = dot(weights.astype(BF16), both)
            parts.append(product[:, :wide] + product[:, wide:])
        y[:, at] = jnp.where(first, parts[0], parts[1]) + values * spread(skips, p)
    fetched["z"].wait()
    fetched["gain"].wait()
    c_high, c_low = split(c_mat)
    c_pair[...] = jnp.concatenate([c_high, c_low], axis=1)
    gate[...] = silu(z_ref[...].astype(F32))

    incoming[...] = jnp.zeros_like(incoming)
    for source in range(n_ctx - 1):

        @pl.when(source < ctx)
        def _():
            pltpu.make_async_copy(
                state_in.at[source], state_in.at[source], state_recv.at[0, source]
            ).wait()
            pltpu.make_async_copy(
                carry_in.at[source], carry_in.at[source], state_recv.at[1, source]
            ).wait()
            incoming[...] = incoming[...] * carry_in[source, 0:1, :] + state_in[source].astype(F32)

    state = incoming[...].astype(BF16)
    states = jnp.concatenate([state, state], axis=0)
    half_rows = length // HALVES

    def half(r):
        return pl.ds(r * half_rows, half_rows)

    def hid_swap(r):
        return remote(
            hid_own.at[half(r)], hid_sib.at[half(r)], hid_send.at[r], hid_recv.at[r], ctx, sib
        )

    for r in range(HALVES):
        carried = dot(c_pair[half(r), :], states)
        gated = (y[half(r), :] + carried * grown[half(r), :]) * gate[half(r), :]
        y[half(r), :] = gated
        hid_own[half(r), :] = (gated * gain_ref[...]).astype(BF16)
        hid_swap(r).start()

    def part(r):
        return pl.ds(r * rows, rows)

    def block_copy(target, r, forward):
        if forward:
            slot, to = target, rank + 2
        else:
            slot, to = jnp.where(target == zed - 1, n_z, target), rank - 2
        return remote(
            outgoing.at[target, part(r)],
            arrived.at[slot, part(r)],
            block_send.at[target, r],
            block_recv.at[slot, r],
            ctx,
            to,
        )

    def block_wait(slot, r):
        pltpu.make_async_copy(
            arrived.at[slot, part(r)], arrived.at[slot, part(r)], block_recv.at[slot, r]
        ).wait()

    for b in range(n_z):
        local_w[b].wait()
        sent_w[b].wait_recv()

    def launch(target, chunks):
        @pl.when((zed == 0) | (zed == n_z - 1))
        def _():
            for r in chunks:
                outgoing[target, part(r)] = acc[target, part(r)].astype(BF16)

        @pl.when(zed == 0)
        def _():
            for r in chunks:
                block_copy(target, r, True).start()

        @pl.when(zed == n_z - 1)
        def _():
            for r in chunks:
                block_copy(target, r, False).start()

    def square_copy(target):
        return remote(
            squares.at[rank],
            squares.at[rank],
            square_send.at[target],
            square_recv.at[rank],
            ctx,
            target,
        )

    upward = zed < n_z // 2
    per_half = CHUNKS // HALVES
    for i in range(n_z):
        target = jnp.where(upward, n_z - 1 - i, i)
        if i == 0:
            for r in range(HALVES):
                own = dot(hid_own[half(r), :], w_own[target])
                hid_swap(r).wait_recv()
                acc[target, half(r)] = own + dot(hid_sib[half(r), :], w_sib[target])
                launch(target, range(r * per_half, (r + 1) * per_half))
        else:
            acc[target] = dot(hid_own[...], w_own[target]) + dot(hid_sib[...], w_sib[target])
            if i < n_z - 1:
                launch(target, range(CHUNKS))

    norm = jnp.sum(y[...] * y[...], axis=1, keepdims=True)
    squares[rank] = jnp.broadcast_to(norm, (length, 128)).T[0:8, :]
    for target in range(n_tp):

        @pl.when(target != rank)
        def _():
            square_copy(target).start()

    def relay(target, r, forward):
        block_wait(target, r)
        outgoing[target, part(r)] = (
            acc[target, part(r)] + arrived[target, part(r)].astype(F32)
        ).astype(BF16)
        block_copy(target, r, forward).start()

    for i in range(n_z - 1):
        for r in range(CHUNKS):

            @pl.when((zed > 0) & (zed < n_z - 1 - i))
            def _():
                relay(n_z - 1 - i, r, True)

            @pl.when((zed < n_z - 1) & (zed > i))
            def _():
                relay(i, r, False)

    for target in range(n_tp):

        @pl.when(target != rank)
        def _():
            pltpu.make_async_copy(
                squares.at[target], squares.at[target], square_recv.at[target]
            ).wait()

    mean = jnp.sum(squares[...], axis=0) * (1.0 / (inner * n_tp))
    scale = lax.rsqrt(mean + 1e-05).T[:, 0:1]
    for r in range(CHUNKS):

        @pl.when(zed < n_z - 1)
        def _():
            block_wait(n_z, r)
            acc[zed, part(r)] = acc[zed, part(r)] + arrived[n_z, part(r)].astype(F32)

        @pl.when(zed > 0)
        def _():
            block_wait(zed, r)
            acc[zed, part(r)] = acc[zed, part(r)] + arrived[zed, part(r)].astype(F32)

        out_ref[part(r), :] = (
            acc[zed, part(r)] * scale[r * rows : (r + 1) * rows, :]
        ).astype(BF16)

    @pl.when(ctx < n_ctx - 1)
    def _():
        x_halo.wait_send()
        bc_halo.wait_send()
        bc_halo_sib.wait_send()

    bc_swap.wait_send()
    for copy in sent_w:
        copy.wait_send()
    for target in range(1, n_ctx):

        @pl.when(target > ctx)
        def _():
            for copy in state_copies(target):
                copy.wait_send()

    for r in range(HALVES):
        hid_swap(r).wait_send()
    for target in range(n_tp):

        @pl.when(target != rank)
        def _():
            square_copy(target).wait_send()

    for target in range(n_z):
        for r in range(CHUNKS):

            @pl.when(zed != target)
            def _():
                pltpu.make_async_copy(
                    outgoing.at[target, part(r)],
                    outgoing.at[target, part(r)],
                    block_send.at[target, r],
                ).wait()


def solution(mesh):
    n_ctx, n_tp = mesh.shape["ctx"], mesh.shape["tp"]
    n_z = n_tp // 2

    def shards(
        x_input,
        z_input,
        bc_input,
        dt_input,
        decay_log,
        skip_weight,
        conv_x,
        conv_bc,
        conv_bias_x,
        conv_bias_bc,
        norm_gain,
        out_weight,
    ):
        length, inner = x_input.shape
        size = bc_input.shape[1]
        heads = dt_input.shape[1]
        features = out_weight.shape[1]
        width = features // n_tp
        vmem = pl.BlockSpec(memory_space=pltpu.VMEM)
        hbm = pl.BlockSpec(memory_space=pl.ANY)
        dma = pltpu.SemaphoreType.DMA
        return pl.pallas_call(
            functools.partial(layer_kernel, n_ctx, n_tp),
            out_shape=jax.ShapeDtypeStruct((length, width), BF16),
            in_specs=[hbm] * 12,
            out_specs=vmem,
            scratch_shapes=[
                pltpu.VMEM((length, inner), BF16),
                pltpu.VMEM((length, inner), BF16),
                pltpu.VMEM((heads, length), F32),
                pltpu.VMEM((1, heads), F32),
                pltpu.VMEM((1, heads), F32),
                pltpu.VMEM((conv_x.shape[0], inner), F32),
                pltpu.VMEM((conv_bc.shape[0], 2 * size), F32),
                pltpu.VMEM((1, inner), F32),
                pltpu.VMEM((1, 2 * size), F32),
                pltpu.VMEM((1, inner), F32),
                dma((11,)),
                pltpu.VMEM((HALO, inner), BF16),
                pltpu.VMEM((2, HALO, size), BF16),
                pltpu.VMEM((2, length, size), BF16),
                pltpu.VMEM((HALO + length, inner), F32),
                pltpu.VMEM((HALO + length, 2 * size), F32),
                pltpu.VMEM((length, inner), F32),
                pltpu.VMEM((length, inner), F32),
                pltpu.VMEM((length, inner), F32),
                pltpu.VMEM((length, inner), F32),
                pltpu.VMEM((length, 2 * size), BF16),
                pltpu.VMEM((size, inner), BF16),
                pltpu.VMEM((8, inner), F32),
                pltpu.VMEM((n_ctx, size, inner), BF16),
                pltpu.VMEM((n_ctx, 8, inner), F32),
                pltpu.VMEM((size, inner), F32),
                pltpu.VMEM((n_tp, 8, length), F32),
                pltpu.VMEM((length, inner), BF16),
                pltpu.VMEM((length, inner), BF16),
                pltpu.VMEM((n_z, inner, width), BF16),
                pltpu.VMEM((n_z, inner, width), BF16),
                pltpu.VMEM((n_z, length, width), F32),
                pltpu.VMEM((n_z, length, width), BF16),
                pltpu.VMEM((n_z + 1, length, width), BF16),
                dma((4,)),
                dma((4,)),
                dma((2, n_ctx)),
                dma((2, n_ctx)),
                dma((n_tp,)),
                dma((n_tp,)),
                dma((HALVES,)),
                dma((HALVES,)),
                dma((n_z,)),
                dma((n_z,)),
                dma((n_z,)),
                dma((n_z, CHUNKS)),
                dma((n_z + 1, CHUNKS)),
            ],
            compiler_params=pltpu.CompilerParams(
                collective_id=0, has_side_effects=True, vmem_limit_bytes=56 * 1024 * 1024
            ),
        )(
            x_input,
            z_input,
            bc_input,
            dt_input.T,
            decay_log.reshape(1, heads),
            skip_weight.reshape(1, heads),
            conv_x,
            conv_bc,
            conv_bias_x.reshape(1, -1),
            conv_bias_bc.reshape(1, -1),
            norm_gain.reshape(1, -1),
            out_weight,
        )

    in_specs = (
        P("ctx", "tp"),
        P("ctx", "tp"),
        P("ctx", "tp"),
        P("ctx", "tp"),
        P("tp"),
        P("tp"),
        P(None, "tp"),
        P(),
        P("tp"),
        P(),
        P("tp"),
        P("tp", None),
    )
    return jax.shard_map(
        shards, mesh=mesh, in_specs=in_specs, out_specs=P("ctx", "tp"), check_vma=False
    )
```

```python
import functools

import jax
import jax.numpy as jnp
from jax import lax
from jax.experimental import pallas as pl
from jax.experimental.pallas import tpu as pltpu
from jax.sharding import PartitionSpec as P

MESH = pl.DeviceIdType.MESH
HIGH = lax.Precision.HIGHEST
F32 = jnp.float32
BF16 = jnp.bfloat16
HALO = 16
CHUNKS = 4
HALVES = 2


def dot(a, b, precision=None):
    return jnp.dot(a, b, preferred_element_type=F32, precision=precision)


def silu(v):
    return v / (1.0 + jnp.exp(-v))


def split(v):
    high = v.astype(BF16)
    return high, (v - high.astype(F32)).astype(BF16)


def layer_kernel(
    n_ctx,
    n_tp,
    x_hbm,
    z_hbm,
    bc_ref,
    dt_hbm,
    decay_hbm,
    skip_hbm,
    conv_x_hbm,
    conv_bc_hbm,
    bias_x_hbm,
    bias_bc_hbm,
    gain_hbm,
    w_ref,
    out_ref,
    x_ref,
    z_ref,
    dt_ref,
    decay_ref,
    skip_ref,
    conv_x_ref,
    conv_bc_ref,
    bias_x_ref,
    bias_bc_ref,
    gain_ref,
    fetch_sem,
    halo_x,
    halo_bc,
    raw_bc,
    pad_x,
    pad_bc,
    xs,
    y,
    grown,
    gate,
    c_pair,
    state_own,
    carry_own,
    state_in,
    carry_in,
    incoming,
    squares,
    hid_own,
    hid_sib,
    w_own,
    w_sib,
    acc,
    outgoing,
    arrived,
    halo_send,
    halo_recv,
    state_send,
    state_recv,
    square_send,
    square_recv,
    hid_send,
    hid_recv,
    w_local,
    w_send,
    w_recv,
    block_send,
    block_recv,
    w_lent,
    hid_lent,
    lend_send,
    lend_recv,
    spread_send,
    spread_recv,
    lent_send,
    lent_recv,
    pass_send,
):
    ctx = lax.axis_index("ctx")
    rank = lax.axis_index("tp")
    zed = rank // 2
    core = rank % 2
    sib = rank + 1 - 2 * core
    n_z = n_tp // 2
    length, inner = x_ref.shape
    size = bc_ref.shape[1]
    heads = dt_ref.shape[0]
    taps = conv_x_ref.shape[0]
    width = w_own.shape[2]
    rows = length // CHUNKS
    wide = 2 * (inner // heads)

    group = pl.ds(pl.multiple_of(zed * 2 * size, 2 * size), 2 * size)
    fetched = {}
    for at, (name, src, dst) in enumerate(
        (
            ("dt", dt_hbm, dt_ref),
            ("decay", decay_hbm, decay_ref),
            ("x", x_hbm, x_ref),
            ("conv_x", conv_x_hbm, conv_x_ref),
            ("bias_x", bias_x_hbm, bias_x_ref),
            ("bc", bc_ref, raw_bc.at[core]),
            ("conv_bc", conv_bc_hbm.at[:, group], conv_bc_ref),
            ("bias_bc", bias_bc_hbm.at[:, group], bias_bc_ref),
            ("skip", skip_hbm, skip_ref),
            ("z", z_hbm, z_ref),
            ("gain", gain_hbm, gain_ref),
        )
    ):
        fetched[name] = pltpu.make_async_copy(src, dst, fetch_sem.at[at])

    barrier = pltpu.get_barrier_semaphore()

    def greet(c, r):
        pl.semaphore_signal(barrier, inc=1, device_id=(c, r), device_id_type=MESH)

    for step in range(1, n_tp):
        greet(ctx, lax.rem(rank + step, n_tp))
    for step in range(1, n_ctx):
        greet(lax.rem(ctx + step, n_ctx), rank)
    greet(lax.rem(ctx + 1, n_ctx), sib)
    greet(lax.rem(ctx + n_ctx - 1, n_ctx), sib)

    for copy in fetched.values():
        copy.start()

    def w_block(block, half):
        return w_ref.at[:, pl.ds(pl.multiple_of((2 * block + half) * width, width), width)]

    def remote(src, dst, send, recv, c, r):
        return pltpu.make_async_remote_copy(
            src_ref=src,
            dst_ref=dst,
            send_sem=send,
            recv_sem=recv,
            device_id=(c, r),
            device_id_type=MESH,
        )

    local_w = [
        pltpu.make_async_copy(w_block(b, core), w_own.at[b], w_local.at[b]) for b in range(n_z)
    ]
    pl.semaphore_wait(barrier, (n_tp - 1) + (n_ctx - 1) + 2)

    later = lax.rem(ctx + 1, n_ctx)
    tail = pl.ds(length - HALO, HALO)
    x_halo = remote(
        x_hbm.at[tail], halo_x, halo_send.at[0], halo_recv.at[0], later, rank
    )
    bc_halo = remote(
        bc_ref.at[tail], halo_bc.at[core], halo_send.at[1], halo_recv.at[1 + core], later, rank
    )
    bc_halo_sib = remote(
        bc_ref.at[tail], halo_bc.at[core], halo_send.at[2], halo_recv.at[1 + core], later, sib
    )
    bc_swap = remote(
        bc_ref, raw_bc.at[core], halo_send.at[3], halo_recv.at[3], ctx, sib
    )

    @pl.when(ctx < n_ctx - 1)
    def _():
        x_halo.start()
        bc_halo.start()
        bc_halo_sib.start()

    bc_swap.start()
    sent_w = [
        remote(w_block(b, 1 - core), w_sib.at[b], w_send.at[b], w_recv.at[b], ctx, sib)
        for b in range(n_z)
    ]
    for b in range(n_z):
        sent_w[b].start()
        local_w[b].start()

    lends = n_z >= 4
    is_end = (zed == 0) | (zed == n_z - 1)
    is_next = (zed == 1) | (zed == n_z - 2)
    inner_zed = jnp.where(zed == 0, 1, n_z - 2)
    share = inner // n_ctx
    own_share = pl.ds(pl.multiple_of(ctx * share, share), share)

    def lend_w(half):
        columns = pl.ds(pl.multiple_of((2 * inner_zed + half) * width, width), width)
        return remote(
            w_ref.at[own_share, columns],
            w_lent.at[core, own_share],
            lend_send.at[half],
            lend_recv.at[core],
            ctx,
            2 * inner_zed + half,
        )

    def spread_w(step):
        return remote(
            w_lent.at[:, own_share],
            w_lent.at[:, own_share],
            spread_send.at[step],
            spread_recv.at[ctx],
            lax.rem(ctx + step, n_ctx),
            rank,
        )

    if lends:

        @pl.when(is_end)
        def _():
            for half in range(2):
                lend_w(half).start()

    fetched["dt"].wait()
    fetched["decay"].wait()
    logits = dt_ref[...]
    step_size = jnp.maximum(logits, 0.0) + jnp.log(1.0 + jnp.exp(-jnp.abs(logits)))
    head_row = lax.broadcasted_iota(jnp.int32, (heads, heads), 0)
    head_lane = lax.broadcasted_iota(jnp.int32, (heads, heads), 1)
    decay = jnp.where(head_row == head_lane, decay_ref[...], 0.0)
    rate = -jnp.exp(jnp.sum(decay, axis=1, keepdims=True))
    earlier = lax.broadcasted_iota(jnp.int32, (length, length), 0)
    after = lax.broadcasted_iota(jnp.int32, (length, length), 1)
    upper = jnp.where(earlier <= after, 1.0, 0.0).astype(F32)
    running = dot(step_size * rate, upper, HIGH)
    total = running[:, length - 1 : length]
    closing = jnp.exp(total - running) * step_size
    running_col = running.T
    closing_col = closing.T
    grown_col = jnp.exp(running_col)
    last_col = grown_col[length - 1 : length, :]
    lane = lax.broadcasted_iota(jnp.int32, (1, wide), 1)
    first = lane < wide // 2

    def spread(cols, pair):
        return jnp.where(
            first, cols[:, 2 * pair : 2 * pair + 1], cols[:, 2 * pair + 1 : 2 * pair + 2]
        )

    pairs = heads // 2
    for p in range(pairs):
        at = slice(p * wide, (p + 1) * wide)
        grown[:, at] = spread(grown_col, p)
        carry_own[:, at] = jnp.broadcast_to(spread(last_col, p), (8, wide))

    def conv(pad, kernel, bias, begin, end):
        value = bias
        for k in range(taps):
            start = HALO - (taps - 1) + k
            value = value + kernel[k : k + 1, :] * pad[start + begin : start + end, :]
        return silu(value)

    fetched["x"].wait()
    fetched["conv_x"].wait()
    fetched["bias_x"].wait()
    pad_x[HALO:, :] = x_ref[...].astype(F32)
    xs[HALO:, :] = conv(pad_x, conv_x_ref[...], bias_x_ref[...], HALO, length)

    @pl.when(ctx == 0)
    def _():
        halo_x[...] = jnp.zeros_like(halo_x)
        halo_bc[...] = jnp.zeros_like(halo_bc)

    @pl.when(ctx > 0)
    def _():
        x_halo.wait_recv()

    pad_x[0:HALO, :] = halo_x[...].astype(F32)
    xs[0:HALO, :] = conv(pad_x, conv_x_ref[...], bias_x_ref[...], 0, HALO)

    @pl.when(ctx > 0)
    def _():
        for half in range(2):
            pltpu.make_async_copy(
                halo_bc.at[half], halo_bc.at[half], halo_recv.at[1 + half]
            ).wait()

    fetched["bc"].wait()
    fetched["conv_bc"].wait()
    fetched["bias_bc"].wait()
    bc_swap.wait_recv()
    for half in range(2):
        at = slice(half * size, (half + 1) * size)
        pad_bc[0:HALO, at] = halo_bc[half].astype(F32)
        pad_bc[HALO:, at] = raw_bc[half].astype(F32)
    bcs = conv(pad_bc, conv_bc_ref[...], bias_bc_ref[...], 0, length)
    b_mat = bcs[:, :size]
    c_mat = bcs[:, size:]

    b_turned = b_mat.T.astype(BF16)
    for p in range(pairs):
        at = slice(p * wide, (p + 1) * wide)
        scaled = (xs[:, at] * spread(closing_col, p)).astype(BF16)
        state_own[:, at] = dot(b_turned, scaled).astype(BF16)

    def state_copies(target):
        return (
            remote(
                state_own,
                state_in.at[ctx],
                state_send.at[0, target],
                state_recv.at[0, ctx],
                target,
                rank,
            ),
            remote(
                carry_own,
                carry_in.at[ctx],
                state_send.at[1, target],
                state_recv.at[1, ctx],
                target,
                rank,
            ),
        )

    for target in range(1, n_ctx):

        @pl.when(target > ctx)
        def _():
            for copy in state_copies(target):
                copy.start()

    meeting = lax.dot_general(
        c_mat, b_mat, (((1,), (1,)), ((), ())), preferred_element_type=F32, precision=HIGH
    )
    fetched["skip"].wait()
    skips = skip_ref[...]
    meeting = jnp.where(earlier >= after, meeting, 0.0)
    for p in range(pairs):
        at = slice(p * wide, (p + 1) * wide)
        values = xs[:, at]
        high, low = split(values)
        both = jnp.concatenate([high, low], axis=1)
        parts = []
        for h in (2 * p, 2 * p + 1):
            gap = running_col[:, h : h + 1] - running[h : h + 1, :]
            weights = jnp.exp(jnp.minimum(gap, 0.0)) * meeting * step_size[h : h + 1, :]
            product = dot(weights.astype(BF16), both)
            parts.append(product[:, :wide] + product[:, wide:])
        y[:, at] = jnp.where(first, parts[0], parts[1]) + values * spread(skips, p)
    fetched["z"].wait()
    fetched["gain"].wait()
    c_high, c_low = split(c_mat)
    c_pair[...] = jnp.concatenate([c_high, c_low], axis=1)
    gate[...] = silu(z_ref[...].astype(F32))

    incoming[...] = jnp.zeros_like(incoming)
    for source in range(n_ctx - 1):

        @pl.when(source < ctx)
        def _():
            pltpu.make_async_copy(
                state_in.at[source], state_in.at[source], state_recv.at[0, source]
            ).wait()
            pltpu.make_async_copy(
                carry_in.at[source], carry_in.at[source], state_recv.at[1, source]
            ).wait()
            incoming[...] = incoming[...] * carry_in[source, 0:1, :] + state_in[source].astype(F32)

    state = incoming[...].astype(BF16)
    states = jnp.concatenate([state, state], axis=0)
    half_rows = length // HALVES

    def half(r):
        return pl.ds(r * half_rows, half_rows)

    def hid_swap(r):
        return remote(
            hid_own.at[half(r)], hid_sib.at[half(r)], hid_send.at[r], hid_recv.at[r], ctx, sib
        )

    def lend_hid(r):
        return remote(
            hid_own.at[half(r)],
            hid_lent.at[core, half(r)],
            lent_send.at[r],
            lent_recv.at[core, r],
            ctx,
            2 * inner_zed + core,
        )

    def pass_hid(r):
        return remote(
            hid_lent.at[core, half(r)],
            hid_lent.at[core, half(r)],
            pass_send.at[r],
            lent_recv.at[core, r],
            ctx,
            sib,
        )

    def lent_wait(source, r):
        pltpu.make_async_copy(
            hid_lent.at[source, half(r)], hid_lent.at[source, half(r)], lent_recv.at[source, r]
        ).wait()

    for r in range(HALVES):
        carried = dot(c_pair[half(r), :], states)
        gated = (y[half(r), :] + carried * grown[half(r), :]) * gate[half(r), :]
        y[half(r), :] = gated
        hid_own[half(r), :] = (gated * gain_ref[...]).astype(BF16)
        hid_swap(r).start()
        if lends:

            @pl.when(is_end)
            def _():
                lend_hid(r).start()

    if lends:

        @pl.when(is_next)
        def _():
            for source in range(2):
                pltpu.make_async_copy(
                    w_lent.at[source, own_share], w_lent.at[source, own_share], lend_recv.at[source]
                ).wait()
            for step in range(1, n_ctx):
                spread_w(step).start()

    def part(r):
        return pl.ds(r * rows, rows)

    def block_copy(target, r, forward):
        if forward:
            slot, to = target, rank + 2
        else:
            slot, to = jnp.where(target == zed - 1, n_z, target), rank - 2
        return remote(
            outgoing.at[target, part(r)],
            arrived.at[slot, part(r)],
            block_send.at[target, r],
            block_recv.at[slot, r],
            ctx,
            to,
        )

    def block_wait(slot, r):
        pltpu.make_async_copy(
            arrived.at[slot, part(r)], arrived.at[slot, part(r)], block_recv.at[slot, r]
        ).wait()

    for b in range(n_z):
        local_w[b].wait()
        sent_w[b].wait_recv()

    def launch(target, chunks):
        @pl.when((zed == 0) | (zed == n_z - 1))
        def _():
            for r in chunks:
                outgoing[target, part(r)] = acc[target, part(r)].astype(BF16)

        @pl.when(zed == 0)
        def _():
            for r in chunks:
                block_copy(target, r, True).start()

        @pl.when(zed == n_z - 1)
        def _():
            for r in chunks:
                block_copy(target, r, False).start()

    def square_copy(target):
        return remote(
            squares.at[rank],
            squares.at[rank],
            square_send.at[target],
            square_recv.at[rank],
            ctx,
            target,
        )

    upward = zed < n_z // 2
    per_half = CHUNKS // HALVES
    for i in range(n_z):
        target = jnp.where(upward, n_z - 1 - i, i)
        if i == 0:
            for r in range(HALVES):
                own = dot(hid_own[half(r), :], w_own[target])
                hid_swap(r).wait_recv()
                acc[target, half(r)] = own + dot(hid_sib[half(r), :], w_sib[target])
                launch(target, range(r * per_half, (r + 1) * per_half))
        elif lends and i == n_z - 2:

            @pl.when(jnp.logical_not(is_end))
            def _():
                acc[target] = dot(hid_own[...], w_own[target]) + dot(hid_sib[...], w_sib[target])

        else:
            acc[target] = dot(hid_own[...], w_own[target]) + dot(hid_sib[...], w_sib[target])
            if i < n_z - 1:
                launch(target, range(CHUNKS))

    norm = jnp.sum(y[...] * y[...], axis=1, keepdims=True)
    squares[rank] = jnp.broadcast_to(norm, (length, 128)).T[0:8, :]
    for target in range(n_tp):

        @pl.when(target != rank)
        def _():
            square_copy(target).start()

    def relay(target, r, forward):
        block_wait(target, r)
        outgoing[target, part(r)] = (
            acc[target, part(r)] + arrived[target, part(r)].astype(F32)
        ).astype(BF16)
        block_copy(target, r, forward).start()

    if lends:

        @pl.when(is_next)
        def _():
            for r in range(HALVES):
                lent_wait(core, r)
                pass_hid(r).start()

    for i in range(n_z - 1):
        for r in range(CHUNKS):

            @pl.when((zed > 0) & (zed < n_z - 1 - i))
            def _():
                relay(n_z - 1 - i, r, True)

            @pl.when((zed < n_z - 1) & (zed > i))
            def _():
                relay(i, r, False)

    for target in range(n_tp):

        @pl.when(target != rank)
        def _():
            pltpu.make_async_copy(
                squares.at[target], squares.at[target], square_recv.at[target]
            ).wait()

    mean = jnp.sum(squares[...], axis=0) * (1.0 / (inner * n_tp))
    scale = lax.rsqrt(mean + 1e-05).T[:, 0:1]
    if lends:

        @pl.when(is_next)
        def _():
            for r in range(HALVES):
                lent_wait(1 - core, r)
            for source in range(n_ctx):

                @pl.when(source != ctx)
                def _():
                    rows_of = pl.ds(source * share, share)
                    pltpu.make_async_copy(
                        w_lent.at[:, rows_of], w_lent.at[:, rows_of], spread_recv.at[source]
                    ).wait()

            acc[zed] = acc[zed] + (
                dot(hid_lent[0], w_lent[0]) + dot(hid_lent[1], w_lent[1])
            )

    from_above = (zed < n_z - 1) & (zed != n_z - 2) if lends else zed < n_z - 1
    from_below = (zed > 0) & (zed != 1) if lends else zed > 0
    for r in range(CHUNKS):

        @pl.when(from_above)
        def _():
            block_wait(n_z, r)
            acc[zed, part(r)] = acc[zed, part(r)] + arrived[n_z, part(r)].astype(F32)

        @pl.when(from_below)
        def _():
            block_wait(zed, r)
            acc[zed, part(r)] = acc[zed, part(r)] + arrived[zed, part(r)].astype(F32)

        out_ref[part(r), :] = (
            acc[zed, part(r)] * scale[r * rows : (r + 1) * rows, :]
        ).astype(BF16)

    @pl.when(ctx < n_ctx - 1)
    def _():
        x_halo.wait_send()
        bc_halo.wait_send()
        bc_halo_sib.wait_send()

    bc_swap.wait_send()
    for copy in sent_w:
        copy.wait_send()
    for target in range(1, n_ctx):

        @pl.when(target > ctx)
        def _():
            for copy in state_copies(target):
                copy.wait_send()

    for r in range(HALVES):
        hid_swap(r).wait_send()
    for target in range(n_tp):

        @pl.when(target != rank)
        def _():
            square_copy(target).wait_send()

    if lends:

        @pl.when(is_end)
        def _():
            for half_at in range(2):
                lend_w(half_at).wait_send()
            for r in range(HALVES):
                lend_hid(r).wait_send()

        @pl.when(is_next)
        def _():
            for step in range(1, n_ctx):
                spread_w(step).wait_send()
            for r in range(HALVES):
                pass_hid(r).wait_send()

    for target in range(n_z):
        for r in range(CHUNKS):

            sent = zed != target
            if lends and target == 1:
                sent = sent & (zed != 0)
            if lends and target == n_z - 2:
                sent = sent & (zed != n_z - 1)

            @pl.when(sent)
            def _():
                pltpu.make_async_copy(
                    outgoing.at[target, part(r)],
                    outgoing.at[target, part(r)],
                    block_send.at[target, r],
                ).wait()


def solution(mesh):
    n_ctx, n_tp = mesh.shape["ctx"], mesh.shape["tp"]
    n_z = n_tp // 2

    def shards(
        x_input,
        z_input,
        bc_input,
        dt_input,
        decay_log,
        skip_weight,
        conv_x,
        conv_bc,
        conv_bias_x,
        conv_bias_bc,
        norm_gain,
        out_weight,
    ):
        length, inner = x_input.shape
        size = bc_input.shape[1]
        heads = dt_input.shape[1]
        features = out_weight.shape[1]
        width = features // n_tp
        vmem = pl.BlockSpec(memory_space=pltpu.VMEM)
        hbm = pl.BlockSpec(memory_space=pl.ANY)
        dma = pltpu.SemaphoreType.DMA
        return pl.pallas_call(
            functools.partial(layer_kernel, n_ctx, n_tp),
            out_shape=jax.ShapeDtypeStruct((length, width), BF16),
            in_specs=[hbm] * 12,
            out_specs=vmem,
            scratch_shapes=[
                pltpu.VMEM((length, inner), BF16),
                pltpu.VMEM((length, inner), BF16),
                pltpu.VMEM((heads, length), F32),
                pltpu.VMEM((1, heads), F32),
                pltpu.VMEM((1, heads), F32),
                pltpu.VMEM((conv_x.shape[0], inner), F32),
                pltpu.VMEM((conv_bc.shape[0], 2 * size), F32),
                pltpu.VMEM((1, inner), F32),
                pltpu.VMEM((1, 2 * size), F32),
                pltpu.VMEM((1, inner), F32),
                dma((11,)),
                pltpu.VMEM((HALO, inner), BF16),
                pltpu.VMEM((2, HALO, size), BF16),
                pltpu.VMEM((2, length, size), BF16),
                pltpu.VMEM((HALO + length, inner), F32),
                pltpu.VMEM((HALO + length, 2 * size), F32),
                pltpu.VMEM((length, inner), F32),
                pltpu.VMEM((length, inner), F32),
                pltpu.VMEM((length, inner), F32),
                pltpu.VMEM((length, inner), F32),
                pltpu.VMEM((length, 2 * size), BF16),
                pltpu.VMEM((size, inner), BF16),
                pltpu.VMEM((8, inner), F32),
                pltpu.VMEM((n_ctx, size, inner), BF16),
                pltpu.VMEM((n_ctx, 8, inner), F32),
                pltpu.VMEM((size, inner), F32),
                pltpu.VMEM((n_tp, 8, length), F32),
                pltpu.VMEM((length, inner), BF16),
                pltpu.VMEM((length, inner), BF16),
                pltpu.VMEM((n_z, inner, width), BF16),
                pltpu.VMEM((n_z, inner, width), BF16),
                pltpu.VMEM((n_z, length, width), F32),
                pltpu.VMEM((n_z, length, width), BF16),
                pltpu.VMEM((n_z + 1, length, width), BF16),
                dma((4,)),
                dma((4,)),
                dma((2, n_ctx)),
                dma((2, n_ctx)),
                dma((n_tp,)),
                dma((n_tp,)),
                dma((HALVES,)),
                dma((HALVES,)),
                dma((n_z,)),
                dma((n_z,)),
                dma((n_z,)),
                dma((n_z, CHUNKS)),
                dma((n_z + 1, CHUNKS)),
                pltpu.VMEM((2, inner, width), BF16),
                pltpu.VMEM((2, length, inner), BF16),
                dma((2,)),
                dma((2,)),
                dma((n_ctx,)),
                dma((n_ctx,)),
                dma((HALVES,)),
                dma((2, HALVES)),
                dma((HALVES,)),
            ],
            compiler_params=pltpu.CompilerParams(
                collective_id=0, has_side_effects=True, vmem_limit_bytes=56 * 1024 * 1024
            ),
        )(
            x_input,
            z_input,
            bc_input,
            dt_input.T,
            decay_log.reshape(1, heads),
            skip_weight.reshape(1, heads),
            conv_x,
            conv_bc,
            conv_bias_x.reshape(1, -1),
            conv_bias_bc.reshape(1, -1),
            norm_gain.reshape(1, -1),
            out_weight,
        )

    in_specs = (
        P("ctx", "tp"),
        P("ctx", "tp"),
        P("ctx", "tp"),
        P("ctx", "tp"),
        P("tp"),
        P("tp"),
        P(None, "tp"),
        P(),
        P("tp"),
        P(),
        P("tp"),
        P("tp", None),
    )
    return jax.shard_map(
        shards, mesh=mesh, in_specs=in_specs, out_specs=P("ctx", "tp"), check_vma=False
    )
```
